32 devices in a mesh: slab: 16 (over z, y, x), tm: 2 (over core).
Axes of the slice: x: 2, y: 2, z: 4, core: 2. Of those that a mesh axis runs over, the one named last changes fastest.
Arguments:
- bold_series: bfloat16 [16, 262144], P('tm', 'slab'), may hold values from -6 to 6
- tile_index: int32 [2, 256], P(None, 'slab'), may hold values from 0 to 143, as said below
- ribbon_weight: bfloat16 [256, 256, 128], P(('slab', 'tm')), may hold values from -0.375 to 0.375
- vertex_area: bfloat16 [32768], P('slab'), may hold values from 0.25 to 4
- requests: int32 [16, 16, 768], P('slab'), may hold values from 0 to 2047
- corner_slot: int32 [3, 32768], P(None, 'slab'), may hold values from 0 to 12287, as said below
- barycentric: float32 [3, 32768], P(None, 'slab'), may hold values from 0.1 to 1
Outputs:
- fslr_series: float32 [16, 32768], P('tm', 'slab')
The draws below stay inside these ranges and needn't reach their ends.
Inputs may be any that keep to these rules, and one draw needn't show every extreme that they name: `tile_index`: the tiles of vertex block g are 2 distinct values in [b * 8, b * 8 + 2 * 8 + 8) with b = g % 16. `corner_slot`: within the 2048 fsLR vertices of one patch, each slot serves at most one corner; the used slots of block set s are its first n slots, where n is 768 for a quarter of the block sets, 384 for half of them and 0 for the rest, and the patch uses exactly 6144 slots.
All inputs are finite; a program needn't handle non-finite values.
Results may differ from the reference program's by a relative error of at most 0.003.
Values may be sent and summed in bfloat16 or wider, within the bound.
A program may use at most 64 MiB of HBM per device.

```python
import math
import jax
import jax.numpy as jnp
from jax import lax

VOX_DEV = 16384
NB_DEV = 16
NF_DEV = 2048
TILE = 128
TK = 2
HALO_T = 8
FRAMES = 16
VOXELS = 262144
NBLK = 256
NVERT = 32768
NFSLR = 32768
CAP = 768
N_SLAB = 16


def draw_tile_index(key, part):
    stride = VOX_DEV // TILE // NB_DEV
    window = 2 * HALO_T + stride
    blocks = NB_DEV * N_SLAB
    scores = jax.random.randint(key, (blocks, window), 0, 1 << 20) * window + jnp.arange(window, dtype=jnp.int32)[None, :]
    top_scores, offsets = lax.top_k(scores, TK)
    base = jnp.arange(blocks, dtype=jnp.int32) % NB_DEV * stride
    return (base[:, None] + offsets).T.astype(jnp.int32)


def draw_corner_slot(key, part):
    mean_load = 3 * NF_DEV // N_SLAB
    capacity = 2 * mean_load
    quarter = N_SLAB // 4
    ranking = jnp.arange(N_SLAB, dtype=jnp.int32)
    profile = jnp.where(ranking < quarter, capacity, jnp.where(ranking < 3 * quarter, mean_load, 0))

    def one_patch(patch_key):
        first_key, second_key = jax.random.split(patch_key)
        order = jax.random.permutation(first_key, N_SLAB)
        counts = profile[order]
        used = jnp.arange(capacity, dtype=jnp.int32)[None, :] < counts[:, None]
        position = jnp.arange(N_SLAB * capacity, dtype=jnp.int32)
        scores = jnp.where(used.reshape(-1), position, position + N_SLAB * capacity)
        ordered = jnp.sort(scores)[:3 * NF_DEV]
        mixing = jax.random.permutation(second_key, 3 * NF_DEV)
        return ordered[mixing].reshape(3, NF_DEV)
    patch_keys = jax.random.split(key, N_SLAB)
    slots = jax.vmap(one_patch)(patch_keys)
    return jnp.transpose(slots, (1, 0, 2)).reshape(3, N_SLAB * NF_DEV).astype(jnp.int32)


def with_ends(array, rng, smallest, largest):
    longest = array.shape.index(max(array.shape))
    spots = []
    for shift in (0, 1):
        where = [jax.random.randint(jax.random.fold_in(rng, axis), (), 0, length) for axis, length in enumerate(array.shape)]
        where[longest] = (where[longest] + shift) % array.shape[longest]
        spots.append(tuple(where))
    return array.at[spots[0]].set(smallest).at[spots[1]].set(largest)


def steps_of(rng, extent, shards, least, top_value):
    factor_of, own = 1.0, jax.random.fold_in(rng, 6)
    for dim, shards_of in shards:
        heights = jnp.exp(jax.random.uniform(jax.random.fold_in(own, dim), (shards_of,), jnp.float32, least / len(shards), top_value / len(shards)))
        factor_of = factor_of * jnp.repeat(heights, extent[dim] // shards_of).reshape([-1 if axis == dim else 1 for axis in range(len(extent))])
    return factor_of


def centred(key, shape, spread, bound, cuts=(), held_as=jnp.bfloat16):
    level = steps_of(key, shape, cuts, -0.22, 0.18) if cuts else 1.0
    entries = jax.random.normal(key, shape, jnp.float32) * spread * level
    return jnp.minimum(jnp.maximum(entries, -bound), bound).astype(held_as)


def setup_inputs(seed: int = 0) -> dict:
    splits = jax.random.split(jax.random.key(seed), 8)
    bold_series = centred(splits[0], (FRAMES, VOXELS), 1.0, 6.0, ((0, 2), (1, 16)))
    tile_index = draw_tile_index(jax.random.fold_in(splits[7], 71), 0)
    ribbon_weight = centred(splits[2], (NBLK, TK * TILE, TILE), (TK * TILE) ** -0.5, 0.375, ((0, 32),))
    vertex_area = jnp.clip(jnp.exp(math.log(4.0) - 2.7725887 * jax.random.uniform(splits[3], (NVERT,), jnp.float32) ** steps_of(splits[3], (NVERT,), ((0, 16),), -0.2, 0.2)), 0.25, 4.0).astype(jnp.bfloat16)
    requests = with_ends(jax.random.randint(splits[4], (N_SLAB, N_SLAB, CAP), 0, NB_DEV * TILE), jax.random.fold_in(splits[4], 1), 0, (NB_DEV * TILE) - 1).astype(jnp.int32)
    corner_slot = draw_corner_slot(jax.random.fold_in(splits[7], 71), 0)
    barycentric = jnp.clip(0.1 + 0.9 * jax.random.uniform(splits[6], (3, NFSLR), jnp.float32) ** steps_of(splits[6], (3, NFSLR), ((1, 16),), -0.2, 0.2), 0.1, 1.0)
    return dict(bold_series=bold_series, tile_index=tile_index, ribbon_weight=ribbon_weight, vertex_area=vertex_area, requests=requests, corner_slot=corner_slot, barycentric=barycentric)


def reference(bold_series, tile_index, ribbon_weight, vertex_area, requests, corner_slot, barycentric):
    vox_tiles = VOX_DEV // TILE
    padded = jnp.pad(bold_series, ((0, 0), (HALO_T * TILE, HALO_T * TILE)))
    voxel_tiles = padded.reshape(FRAMES, -1, TILE)
    owner = jnp.arange(NB_DEV * N_SLAB, dtype=jnp.int32) // NB_DEV
    global_tile = (owner * vox_tiles)[None, :] + tile_index
    tile_sets = global_tile.T.reshape(N_SLAB, NB_DEV, TK)
    weight_sets = ribbon_weight.reshape(N_SLAB, NB_DEV, TK, TILE, TILE)

    def sample_slab(pair):
        indices, weights = pair
        picked = voxel_tiles[:, indices]
        result = jnp.einsum("fbku,bkuv->fbv", picked.astype(jnp.float32), weights.astype(jnp.float32))
        return result.reshape(FRAMES, NB_DEV * TILE)

    native = lax.map(sample_slab, (tile_sets, weight_sets))
    native = jnp.transpose(native, (1, 0, 2)).reshape(FRAMES, -1).astype(jnp.bfloat16)
    source = corner_slot // CAP
    patch = jnp.arange(N_SLAB * NF_DEV, dtype=jnp.int32) // NF_DEV
    flat_requests = requests.reshape(N_SLAB, N_SLAB * CAP)
    picked_rows = flat_requests[patch[None, :], corner_slot]
    corner = source * (NB_DEV * TILE) + picked_rows
    corner_weight = barycentric * vertex_area[corner].astype(jnp.float32)
    numerator = jnp.zeros((FRAMES, N_SLAB * NF_DEV), jnp.float32)
    for which in range(3):
        numerator = numerator + corner_weight[which][None, :] * native[:, corner[which]].astype(jnp.float32)
    return numerator / jnp.sum(corner_weight, axis=0)[None, :]
```

```python
import functools

import jax
import jax.numpy as jnp
from jax import lax
from jax.experimental import pallas as pl
from jax.experimental.pallas import tpu as pltpu
from jax.sharding import PartitionSpec as P

HALO_T = 8
LANES = 128
MESH = pl.DeviceIdType.MESH


def pick(table, lanes):
    return jnp.take_along_axis(table, lanes, axis=1, mode="promise_in_bounds")


def exchange_kernel(n, m, vregs, tidx, bold, w, area, req, vals, areas, ext, wall, nat, rq, out_buf,
                    halo_s, halo_r, w_s, w_r, rq_s, rq_r, ar_s, ar_r, va_s, va_r):
    me = lax.axis_index("slab")
    t = lax.axis_index("tm")
    tiles = bold.shape[1] // LANES
    own = w.shape[0]
    frames = bold.shape[0]
    blocks = nat.shape[0]
    half = vregs // 2
    halo = HALO_T

    barrier = pltpu.get_barrier_semaphore()

    @pl.loop(1, n)
    def _(r):
        pl.semaphore_signal(barrier, inc=1, device_id={"slab": lax.rem(me + r, n)}, device_id_type=MESH)

    for q in range(1, m):
        pl.semaphore_signal(barrier, inc=1, device_id={"tm": lax.rem(t + q, m)}, device_id_type=MESH)

    def widen(lo, hi):
        for i in range(lo, hi):
            ext[halo + i] = bold[:, i * LANES:(i + 1) * LANES].astype(jnp.float32)

    widen(0, halo)
    widen(tiles - halo, tiles)

    @pl.when(me == 0)
    def _():
        ext[0:halo] = jnp.zeros((halo, frames, LANES), jnp.float32)

    @pl.when(me == n - 1)
    def _():
        ext[halo + tiles:] = jnp.zeros((halo, frames, LANES), jnp.float32)

    pl.semaphore_wait(barrier, n - 1 + m - 1)

    to_right = pltpu.make_async_remote_copy(
        src_ref=ext.at[pl.ds(tiles, halo)], dst_ref=ext.at[pl.ds(0, halo)],
        send_sem=halo_s.at[0], recv_sem=halo_r.at[0],
        device_id={"slab": lax.rem(me + 1, n)}, device_id_type=MESH)
    to_left = pltpu.make_async_remote_copy(
        src_ref=ext.at[pl.ds(halo, halo)], dst_ref=ext.at[pl.ds(halo + tiles, halo)],
        send_sem=halo_s.at[1], recv_sem=halo_r.at[1],
        device_id={"slab": lax.rem(me + n - 1, n)}, device_id_type=MESH)

    @pl.when(me < n - 1)
    def _():
        to_right.start()

    @pl.when(me > 0)
    def _():
        to_left.start()

    def weights_copy(q, owner):
        return pltpu.make_async_remote_copy(
            src_ref=w, dst_ref=wall.at[pl.ds(owner * own, own)],
            send_sem=w_s.at[q], recv_sem=w_r.at[q],
            device_id={"tm": lax.rem(t + q, m)}, device_id_type=MESH)

    for q in range(1, m):
        weights_copy(q, t).start()

    def request_copy(r, to, slot):
        return pltpu.make_async_remote_copy(
            src_ref=req.at[to], dst_ref=rq.at[slot], send_sem=rq_s.at[r], recv_sem=rq_r.at[r],
            device_id={"slab": to}, device_id_type=MESH)

    def area_copy(r, to, slot):
        return pltpu.make_async_remote_copy(
            src_ref=area, dst_ref=areas.at[slot], send_sem=ar_s.at[r], recv_sem=ar_r.at[r],
            device_id={"slab": to}, device_id_type=MESH)

    def value_copy(r, to, slot):
        return pltpu.make_async_remote_copy(
            src_ref=out_buf.at[to], dst_ref=vals.at[slot], send_sem=va_s.at[r], recv_sem=va_r.at[r],
            device_id={"slab": to}, device_id_type=MESH)

    @pl.loop(1, n)
    def _(r):
        request_copy(r, lax.rem(me + r, n), me).start()

    @pl.loop(1, n)
    def _(r):
        area_copy(r, lax.rem(me + r, n), me).start()

    widen(halo, tiles - halo)
    areas[me] = area[...]

    @pl.when(me > 0)
    def _():
        to_right.wait_recv()

    @pl.when(me < n - 1)
    def _():
        to_left.wait_recv()

    def native_block(block, weights):
        x = jnp.concatenate([ext[tidx[k, block]] for k in range(2)], axis=1).astype(jnp.bfloat16)
        y = jnp.dot(x, weights, preferred_element_type=jnp.float32)
        nat[block] = y.astype(jnp.bfloat16).astype(jnp.float32)

    for i in range(own):
        native_block(t * own + i, w[i])
    for q in range(1, m):
        owner = lax.rem(t + m - q, m)
        weights_copy(q, owner).wait_recv()
        for i in range(own):
            native_block(owner * own + i, wall[owner * own + i])

    table = [nat[h] for h in range(blocks)]

    def selected(wanted):
        found = []
        for v in range(vregs):
            row = jnp.broadcast_to(wanted[v:v + 1], (frames, LANES))
            lo, hi = row & (LANES - 1), row >> 7
            acc = pick(table[0], lo)
            for h in range(1, blocks):
                acc = jnp.where(hi == h, pick(table[h], lo), acc)
            found.append(acc)
        return [jnp.concatenate([found[v], found[half + v]], axis=0).astype(jnp.bfloat16) for v in range(half)]

    @pl.loop(1, n)
    def _(r):
        to = lax.rem(me + r, n)
        request_copy(n - r, to, to).wait_recv()
        for v, piece in enumerate(selected(rq[to])):
            out_buf[to, :, v * LANES:(v + 1) * LANES] = piece
        value_copy(r, to, me).start()

    for v, piece in enumerate(selected(req[me])):
        vals[me, :, v * LANES:(v + 1) * LANES] = piece

    @pl.loop(1, n)
    def _(r):
        source = lax.rem(me + n - r, n)
        area_copy(r, source, source).wait_recv()
        value_copy(r, source, source).wait_recv()

    @pl.loop(1, n)
    def _(r):
        to = lax.rem(me + r, n)
        request_copy(r, to, me).wait_send()
        area_copy(r, to, me).wait_send()
        value_copy(r, to, me).wait_send()

    for q in range(1, m):
        weights_copy(q, t).wait_send()

    @pl.when(me < n - 1)
    def _():
        to_right.wait_send()

    @pl.when(me > 0)
    def _():
        to_left.wait_send()


def corners_kernel(cap, vregs, vals, areas, req, slot, bary, out, tbl, area_at, lo_ref, hi_ref, fac):
    n = vals.shape[0]
    rows = areas.shape[1]
    half = vregs // 2
    for s in range(n):
        for v in range(half):
            both = vals[s, :, v * LANES:(v + 1) * LANES].astype(jnp.float32)
            tbl[s * vregs + v] = both[:8]
            tbl[s * vregs + half + v] = both[8:]

    @pl.loop(0, n)
    def _(s):
        wanted = req[s]
        lo, hi = wanted & (LANES - 1), wanted >> 7
        a = areas[s].astype(jnp.float32)
        acc = jnp.zeros((8, LANES), jnp.float32)
        for h in range(rows):
            acc = jnp.where(hi == h, pick(jnp.broadcast_to(a[h:h + 1], (8, LANES)), lo), acc)
        area_at[s] = acc

    flat = slot[...]
    if cap % LANES == 0 and cap == vregs * LANES:
        lo_ref[...] = flat & (LANES - 1)
        hi_ref[...] = flat >> 7
    else:
        source = ((flat.astype(jnp.float32) + 0.5) * (1.0 / cap)).astype(jnp.int32)
        rest = flat - source * cap
        lo_ref[...] = rest & (LANES - 1)
        hi_ref[...] = source * vregs + (rest >> 7)

    @pl.loop(0, slot.shape[0] // 8)
    def _(b):
        at = pl.ds(pl.multiple_of(b * 8, 8), 8)
        lo, hi = lo_ref[at], hi_ref[at]
        acc = jnp.zeros((8, LANES), jnp.float32)
        for s in range(n):
            found = area_at[s]
            for v in range(vregs):
                row = jnp.broadcast_to(found[v:v + 1], (8, LANES))
                acc = jnp.where(hi == s * vregs + v, pick(row, lo), acc)
        fac[at] = bary[at] * acc

    per = slot.shape[0] // 3

    @pl.loop(0, per)
    def _(g):
        lo = [jnp.broadcast_to(lo_ref[pl.ds(k * per + g, 1)], (8, LANES)) for k in range(3)]
        hi = [jnp.broadcast_to(hi_ref[pl.ds(k * per + g, 1)], (8, LANES)) for k in range(3)]
        f = [fac[pl.ds(k * per + g, 1)] for k in range(3)]
        acc = [jnp.zeros((8, LANES), jnp.float32)] * 3
        for e in range(n * vregs):
            here = tbl[e]
            for k in range(3):
                acc[k] = jnp.where(hi[k] == e, pick(here, lo[k]), acc[k])
        top = sum(jnp.broadcast_to(f[k], (8, LANES)) * acc[k] for k in range(3))
        total = jnp.broadcast_to(f[0] + f[1] + f[2], (8, LANES))
        out[:, pl.ds(pl.multiple_of(g * LANES, LANES), LANES)] = top / total


def shards(bold, tile_index, weights, area, requests, slot, bary):
    n, m = lax.axis_size("slab"), lax.axis_size("tm")
    frames = bold.shape[0]
    cap = requests.shape[2]
    vregs = 2 * (-(-cap // (2 * LANES)))
    own, depth, tile = weights.shape
    blocks = own * m
    vmem = pl.BlockSpec(memory_space=pltpu.VMEM)
    smem = pl.BlockSpec(memory_space=pltpu.SMEM)
    req = jnp.pad(requests[0], ((0, 0), (0, 8 * LANES - cap))).reshape(n, 8, LANES)
    sem = lambda k: pltpu.SemaphoreType.DMA((k,))
    vals, areas = pl.pallas_call(
        functools.partial(exchange_kernel, n, m, vregs),
        out_shape=(
            jax.ShapeDtypeStruct((n, 2 * frames, vregs // 2 * LANES), jnp.bfloat16),
            jax.ShapeDtypeStruct((n, area.shape[0] // LANES, LANES), jnp.bfloat16),
        ),
        in_specs=[smem, vmem, vmem, vmem, vmem],
        out_specs=(vmem, vmem),
        scratch_shapes=[
            pltpu.VMEM((bold.shape[1] // LANES + 2 * HALO_T, frames, LANES), jnp.float32),
            pltpu.VMEM((blocks, depth, tile), jnp.bfloat16),
            pltpu.VMEM((blocks, frames, LANES), jnp.float32),
            pltpu.VMEM((n, 8, LANES), jnp.int32),
            pltpu.VMEM((n, 2 * frames, vregs // 2 * LANES), jnp.bfloat16),
            sem(2), sem(2), sem(m), sem(m), sem(n), sem(n), sem(n), sem(n), sem(n), sem(n),
        ],
        compiler_params=pltpu.CompilerParams(
            collective_id=0, has_side_effects=True, vmem_limit_bytes=24 * 2 ** 20),
        name="exchange",
    )(tile_index, bold, weights, area.reshape(-1, LANES), req)
    rows = 3 * slot.shape[1] // LANES
    return pl.pallas_call(
        functools.partial(corners_kernel, cap, vregs),
        out_shape=jax.ShapeDtypeStruct((frames, slot.shape[1]), jnp.float32),
        in_specs=[vmem] * 5,
        out_specs=vmem,
        scratch_shapes=[
            pltpu.VMEM((n * vregs, 8, LANES), jnp.float32),
            pltpu.VMEM((n, 8, LANES), jnp.float32),
            pltpu.VMEM((rows, LANES), jnp.int32),
            pltpu.VMEM((rows, LANES), jnp.int32),
            pltpu.VMEM((rows, LANES), jnp.float32),
        ],
        compiler_params=pltpu.CompilerParams(vmem_limit_bytes=24 * 2 ** 20),
        name="corners",
    )(vals, areas, req, slot.reshape(rows, LANES), bary.reshape(rows, LANES))


def solution(mesh):
    placed = (
        P("tm", "slab"),
        P(None, "slab"),
        P(("slab", "tm"), None, None),
        P("slab"),
        P("slab", None, None),
        P(None, "slab"),
        P(None, "slab"),
    )
    return jax.shard_map(
        shards, mesh=mesh, in_specs=placed, out_specs=P("tm", "slab"), check_vma=False
    )
```

```python
import functools

import jax
import jax.numpy as jnp
from jax import lax
from jax.experimental import pallas as pl
from jax.experimental.pallas import tpu as pltpu
from jax.sharding import PartitionSpec as P

HALO_T = 8
LANES = 128
MESH = pl.DeviceIdType.MESH


def pick(table, lanes):
    return jnp.take_along_axis(table, lanes, axis=1, mode="promise_in_bounds")


def one_hot(lo):
    rows = lax.broadcasted_iota(jnp.int32, (LANES, lo.shape[1]), 0)
    return jnp.where(rows == lo, 1.0, 0.0).astype(jnp.bfloat16)


def exchange_kernel(n, m, vregs, tidx, bold_in, w, area, wanted_in, vals, area_at, ext, wall, nat, req, rq, areas, out_buf,
                    bold, wanted, in_s, halo_s, halo_r, w_s, w_r, rq_s, rq_r, ar_s, ar_r, va_s, va_r):
    me = lax.axis_index("slab")
    t = lax.axis_index("tm")
    tiles = bold.shape[1] // LANES
    own = w.shape[0]
    frames = bold.shape[0]
    blocks = nat.shape[0]
    half = vregs // 2
    halo = HALO_T
    cap = wanted.shape[1]

    load_bold = pltpu.make_async_copy(bold_in, bold, in_s.at[0])
    load_wanted = pltpu.make_async_copy(wanted_in, wanted, in_s.at[1])
    load_area = pltpu.make_async_copy(area, areas.at[me], in_s.at[2])
    mine = pltpu.make_async_copy(w, wall.at[pl.ds(t * own, own)], w_s.at[0])
    load_bold.start()
    load_wanted.start()
    load_area.start()
    mine.start()
    barrier = pltpu.get_barrier_semaphore()

    @pl.loop(1, n)
    def _(r):
        pl.semaphore_signal(barrier, inc=1, device_id={"slab": lax.rem(me + r, n)}, device_id_type=MESH)

    for q in range(1, m):
        pl.semaphore_signal(barrier, inc=1, device_id={"tm": lax.rem(t + q, m)}, device_id_type=MESH)

    load_bold.wait()

    def widen(lo, hi):
        for i in range(lo, hi):
            ext[halo + i] = bold[:, i * LANES:(i + 1) * LANES].astype(jnp.float32)

    widen(0, halo)
    widen(tiles - halo, tiles)

    @pl.when(me == 0)
    def _():
        ext[0:halo] = jnp.zeros((halo, frames, LANES), jnp.float32)

    @pl.when(me == n - 1)
    def _():
        ext[halo + tiles:] = jnp.zeros((halo, frames, LANES), jnp.float32)

    load_wanted.wait()
    req[...] = jnp.zeros(req.shape, jnp.int32)
    for s in range(n):
        for v in range(vregs):
            size = min(LANES, cap - v * LANES)
            if size > 0:
                req[s, v:v + 1, 0:size] = wanted[s:s + 1, v * LANES:v * LANES + size]

    pl.semaphore_wait(barrier, n - 1 + m - 1)

    def weights_copy(q, owner):
        return pltpu.make_async_remote_copy(
            src_ref=w, dst_ref=wall.at[pl.ds(owner * own, own)],
            send_sem=w_s.at[q], recv_sem=w_r.at[q],
            device_id={"tm": lax.rem(t + q, m)}, device_id_type=MESH)

    for q in range(1, m):
        weights_copy(q, t).start()

    to_right = pltpu.make_async_remote_copy(
        src_ref=ext.at[pl.ds(tiles, halo)], dst_ref=ext.at[pl.ds(0, halo)],
        send_sem=halo_s.at[0], recv_sem=halo_r.at[0],
        device_id={"slab": lax.rem(me + 1, n)}, device_id_type=MESH)
    to_left = pltpu.make_async_remote_copy(
        src_ref=ext.at[pl.ds(halo, halo)], dst_ref=ext.at[pl.ds(halo + tiles, halo)],
        send_sem=halo_s.at[1], recv_sem=halo_r.at[1],
        device_id={"slab": lax.rem(me + n - 1, n)}, device_id_type=MESH)

    @pl.when(me < n - 1)
    def _():
        to_right.start()

    @pl.when(me > 0)
    def _():
        to_left.start()

    def request_copy(r, to, slot):
        return pltpu.make_async_remote_copy(
            src_ref=req.at[to], dst_ref=rq.at[slot], send_sem=rq_s.at[r], recv_sem=rq_r.at[r],
            device_id={"slab": to}, device_id_type=MESH)

    def area_copy(r, to, slot):
        return pltpu.make_async_remote_copy(
            src_ref=area, dst_ref=areas.at[slot], send_sem=ar_s.at[r], recv_sem=ar_r.at[r],
            device_id={"slab": to}, device_id_type=MESH)

    def value_copy(r, to, slot):
        return pltpu.make_async_remote_copy(
            src_ref=out_buf.at[to], dst_ref=vals.at[slot], send_sem=va_s.at[r], recv_sem=va_r.at[r],
            device_id={"slab": to}, device_id_type=MESH)

    @pl.loop(1, n)
    def _(r):
        request_copy(r, lax.rem(me + r, n), me).start()

    @pl.loop(1, n)
    def _(r):
        area_copy(r, lax.rem(me + r, n), me).start()

    widen(halo, tiles - halo)
    load_area.wait()
    mine.wait()

    @pl.when(me > 0)
    def _():
        to_right.wait_recv()

    @pl.when(me < n - 1)
    def _():
        to_left.wait_recv()

    for q in range(m):
        owner = lax.rem(t + m - q, m)
        if q:
            weights_copy(q, owner).wait_recv()
        for i in range(own):
            block = owner * own + i
            x = jnp.concatenate([ext[tidx[k, block]] for k in range(2)], axis=1).astype(jnp.bfloat16)
            nat[block] = jnp.dot(x, wall[block], preferred_element_type=jnp.float32)

    table = nat[...].reshape(blocks * frames, LANES).astype(jnp.bfloat16)

    def selected(rows, put):
        for v in range(half):
            row = jnp.concatenate([rows[v:v + 1], rows[half + v:half + v + 1]], axis=1)
            lo = row & (LANES - 1)
            hi = jnp.broadcast_to(row >> 7, (frames, 2 * LANES))
            found = jnp.dot(table, one_hot(lo), preferred_element_type=jnp.float32)
            acc = found[:frames]
            for h in range(1, blocks):
                acc = jnp.where(hi == h, found[h * frames:(h + 1) * frames], acc)
            put(v, jnp.concatenate([acc[:, :LANES], acc[:, LANES:]], axis=0).astype(jnp.bfloat16))

    @pl.loop(1, n)
    def _(r):
        to = lax.rem(me + r, n)
        request_copy(n - r, to, to).wait_recv()

        def put(v, piece):
            out_buf[to, v * 16:(v + 1) * 16, :] = piece

        selected(rq[to], put)
        value_copy(r, to, me).start()

    def put_own(v, piece):
        vals[me, v * 16:(v + 1) * 16, :] = piece

    selected(req[me], put_own)

    @pl.loop(1, n)
    def _(r):
        source = lax.rem(me + n - r, n)
        area_copy(r, source, source).wait_recv()

    @pl.loop(0, n)
    def _(s):
        rows = req[s]
        lo, hi = rows & (LANES - 1), rows >> 7
        a = areas[s].astype(jnp.float32)
        acc = jnp.zeros((8, LANES), jnp.float32)
        for h in range(blocks):
            acc = jnp.where(hi == h, pick(jnp.broadcast_to(a[h:h + 1], (8, LANES)), lo), acc)
        area_at[s] = acc

    @pl.loop(1, n)
    def _(r):
        source = lax.rem(me + n - r, n)
        value_copy(r, source, source).wait_recv()

    @pl.loop(1, n)
    def _(r):
        to = lax.rem(me + r, n)
        request_copy(r, to, me).wait_send()
        area_copy(r, to, me).wait_send()
        value_copy(r, to, me).wait_send()

    for q in range(1, m):
        weights_copy(q, t).wait_send()

    @pl.when(me < n - 1)
    def _():
        to_right.wait_send()

    @pl.when(me > 0)
    def _():
        to_left.wait_send()


def corners_kernel(cap, vregs, vals, area_at, slot, bary, out, tbl, packed):
    n = area_at.shape[0]
    half = vregs // 2
    frames = out.shape[0]
    entries = n * vregs
    width = 2 * LANES
    tbl[:entries * frames] = vals[...]
    for s in range(n):
        packed[s * vregs:(s + 1) * vregs] = area_at[s, :vregs]
    tbl[entries * frames:] = packed[...].astype(jnp.bfloat16)

    @pl.loop(0, out.shape[1] // width)
    def _(g):
        at = pl.ds(pl.multiple_of(g * width, width), width)
        top = jnp.zeros((frames, width), jnp.float32)
        total = jnp.zeros((1, width), jnp.float32)
        for k in range(3):
            flat = slot[k:k + 1, at]
            if cap == vregs * LANES:
                lo, hi = flat & (LANES - 1), flat >> 7
            else:
                source = ((flat.astype(jnp.float32) + 0.5) * (1.0 / cap)).astype(jnp.int32)
                rest = flat - source * cap
                lo, hi = rest & (LANES - 1), source * vregs + (rest >> 7)
            found = jnp.dot(tbl[...], one_hot(lo), preferred_element_type=jnp.float32)
            wide = jnp.broadcast_to(hi, (frames, width))
            acc = jnp.zeros((frames, width), jnp.float32)
            for s in range(n):
                for v in range(half):
                    for j in range(2):
                        e = (s * half + v) * 2 + j
                        here = found[e * frames:(e + 1) * frames]
                        acc = jnp.where(wide == s * vregs + j * half + v, here, acc)
            row8 = lax.broadcasted_iota(jnp.int32, (8, width), 0)
            spread = jnp.zeros((8, width), jnp.float32)
            for b in range(entries // 8):
                at8 = entries * frames + b * 8
                spread = jnp.where(wide == row8 + b * 8, found[at8:at8 + 8], spread)
            factor = bary[k:k + 1, at] * jnp.sum(spread, axis=0, keepdims=True)
            top = top + factor * acc
            total = total + factor
        out[:, at] = top / total


def shards(bold, tile_index, weights, area, requests, slot, bary):
    n, m = lax.axis_size("slab"), lax.axis_size("tm")
    frames = bold.shape[0]
    cap = requests.shape[2]
    vregs = 2 * (-(-cap // (2 * LANES)))
    own, depth, tile = weights.shape
    blocks = own * m
    message = vregs * frames
    entries = n * vregs
    vmem = pl.BlockSpec(memory_space=pltpu.VMEM)
    hbm = pl.BlockSpec(memory_space=pltpu.HBM)
    smem = pl.BlockSpec(memory_space=pltpu.SMEM)
    sem = lambda k: pltpu.SemaphoreType.DMA((k,))
    vals, area_at = pl.pallas_call(
        functools.partial(exchange_kernel, n, m, vregs),
        out_shape=(
            jax.ShapeDtypeStruct((n, message, LANES), jnp.bfloat16),
            jax.ShapeDtypeStruct((n, 8, LANES), jnp.float32),
        ),
        in_specs=[smem, hbm, hbm, hbm, hbm],
        out_specs=(vmem, vmem),
        scratch_shapes=[
            pltpu.VMEM((bold.shape[1] // LANES + 2 * HALO_T, frames, LANES), jnp.float32),
            pltpu.VMEM((blocks, depth, tile), jnp.bfloat16),
            pltpu.VMEM((blocks, frames, LANES), jnp.float32),
            pltpu.VMEM((n, 8, LANES), jnp.int32),
            pltpu.VMEM((n, 8, LANES), jnp.int32),
            pltpu.VMEM((n, area.shape[0] // LANES, LANES), jnp.bfloat16),
            pltpu.VMEM((n, message, LANES), jnp.bfloat16),
            pltpu.VMEM(bold.shape, jnp.bfloat16),
            pltpu.VMEM((n, cap), jnp.int32),
            sem(3), sem(2), sem(2), sem(m), sem(m), sem(n), sem(n), sem(n), sem(n), sem(n), sem(n),
        ],
        compiler_params=pltpu.CompilerParams(
            collective_id=0, has_side_effects=True),
        name="exchange",
    )(tile_index, bold, weights, area.reshape(-1, LANES), requests.reshape(n, cap))
    return pl.pallas_call(
        functools.partial(corners_kernel, cap, vregs),
        out_shape=jax.ShapeDtypeStruct((frames, slot.shape[1]), jnp.float32),
        in_specs=[vmem] * 4,
        out_specs=vmem,
        scratch_shapes=[
            pltpu.VMEM((entries * (frames + 1), LANES), jnp.bfloat16),
            pltpu.VMEM((entries, LANES), jnp.float32),
        ],
        compiler_params=pltpu.CompilerParams(vmem_limit_bytes=24 * 2 ** 20),
        name="corners",
    )(vals.reshape(n * message, LANES), area_at, slot, bary)


def solution(mesh):
    placed = (
        P("tm", "slab"),
        P(None, "slab"),
        P(("slab", "tm"), None, None),
        P("slab"),
        P("slab", None, None),
        P(None, "slab"),
        P(None, "slab"),
    )
    return jax.shard_map(
        shards, mesh=mesh, in_specs=placed, out_specs=P("tm", "slab"), check_vma=False
    )
```

```python
import functools

import jax
import jax.numpy as jnp
from jax import lax
from jax.experimental import pallas as pl
from jax.experimental.pallas import tpu as pltpu
from jax.sharding import PartitionSpec as P

HALO_T = 8
GROUP = 4
LANES = 128
MESH = pl.DeviceIdType.MESH


def pick(table, lanes):
    return jnp.take_along_axis(table, lanes, axis=1, mode="promise_in_bounds")


def one_hot(lo):
    rows = lax.broadcasted_iota(jnp.int32, (LANES, lo.shape[1]), 0)
    return jnp.where(rows == lo, 1.0, 0.0).astype(jnp.bfloat16)


def exchange_kernel(n, m, vregs, tidx, bold_in, w, area, wanted_in, slot_in, bary_in, out, vals, area_at, ext, wall, nat,
                    req, rq, areas, out_buf, bold, wanted, slot, bary, tbl, packed, in_s, halo_s, halo_r, w_s, w_r, rq_s, rq_r, ar_s, ar_r, va_s, va_r):
    me = lax.axis_index("slab")
    t = lax.axis_index("tm")
    tiles = bold.shape[1] // LANES
    own = w.shape[0]
    frames = bold.shape[0]
    blocks = nat.shape[0]
    half = vregs // 2
    halo = HALO_T
    cap = wanted.shape[1]

    load_bold = pltpu.make_async_copy(bold_in, bold, in_s.at[0])
    load_wanted = pltpu.make_async_copy(wanted_in, wanted, in_s.at[1])
    load_area = pltpu.make_async_copy(area, areas.at[me], in_s.at[2])
    mine = pltpu.make_async_copy(w, wall.at[pl.ds(t * own, own)], w_s.at[0])
    load_slot = pltpu.make_async_copy(slot_in, slot, in_s.at[3])
    load_bary = pltpu.make_async_copy(bary_in, bary, in_s.at[4])
    load_bold.start()
    load_wanted.start()
    load_area.start()
    mine.start()
    load_slot.start()
    load_bary.start()
    barrier = pltpu.get_barrier_semaphore()

    @pl.loop(1, n)
    def _(r):
        pl.semaphore_signal(barrier, inc=1, device_id={"slab": lax.rem(me + r, n)}, device_id_type=MESH)

    for q in range(1, m):
        pl.semaphore_signal(barrier, inc=1, device_id={"tm": lax.rem(t + q, m)}, device_id_type=MESH)

    load_bold.wait()

    def widen(lo, hi):
        for i in range(lo, hi):
            ext[halo + i] = bold[:, i * LANES:(i + 1) * LANES].astype(jnp.float32)

    widen(0, halo)
    widen(tiles - halo, tiles)

    @pl.when(me == 0)
    def _():
        ext[0:halo] = jnp.zeros((halo, frames, LANES), jnp.float32)

    @pl.when(me == n - 1)
    def _():
        ext[halo + tiles:] = jnp.zeros((halo, frames, LANES), jnp.float32)

    load_wanted.wait()
    req[...] = jnp.zeros(req.shape, jnp.int32)
    for s in range(n):
        for v in range(vregs):
            size = min(LANES, cap - v * LANES)
            if size > 0:
                req[s, v:v + 1, 0:size] = wanted[s:s + 1, v * LANES:v * LANES + size]

    pl.semaphore_wait(barrier, n - 1 + m - 1)

    def weights_copy(q, owner):
        return pltpu.make_async_remote_copy(
            src_ref=w, dst_ref=wall.at[pl.ds(owner * own, own)],
            send_sem=w_s.at[q], recv_sem=w_r.at[q],
            device_id={"tm": lax.rem(t + q, m)}, device_id_type=MESH)

    for q in range(1, m):
        weights_copy(q, t).start()

    to_right = pltpu.make_async_remote_copy(
        src_ref=ext.at[pl.ds(tiles, halo)], dst_ref=ext.at[pl.ds(0, halo)],
        send_sem=halo_s.at[0], recv_sem=halo_r.at[0],
        device_id={"slab": lax.rem(me + 1, n)}, device_id_type=MESH)
    to_left = pltpu.make_async_remote_copy(
        src_ref=ext.at[pl.ds(halo, halo)], dst_ref=ext.at[pl.ds(halo + tiles, halo)],
        send_sem=halo_s.at[1], recv_sem=halo_r.at[1],
        device_id={"slab": lax.rem(me + n - 1, n)}, device_id_type=MESH)

    @pl.when(me < n - 1)
    def _():
        to_right.start()

    @pl.when(me > 0)
    def _():
        to_left.start()

    def request_copy(r, to, slot):
        return pltpu.make_async_remote_copy(
            src_ref=req.at[to], dst_ref=rq.at[slot], send_sem=rq_s.at[r], recv_sem=rq_r.at[r],
            device_id={"slab": to}, device_id_type=MESH)

    def area_copy(r, to, slot):
        return pltpu.make_async_remote_copy(
            src_ref=area, dst_ref=areas.at[slot], send_sem=ar_s.at[r], recv_sem=ar_r.at[r],
            device_id={"slab": to}, device_id_type=MESH)

    def value_copy(r, to, slot):
        return pltpu.make_async_remote_copy(
            src_ref=out_buf.at[to], dst_ref=vals.at[slot], send_sem=va_s.at[r], recv_sem=va_r.at[r],
            device_id={"slab": to}, device_id_type=MESH)

    @pl.loop(1, n)
    def _(r):
        request_copy(r, lax.rem(me + r, n), me).start()

    @pl.loop(1, n)
    def _(r):
        area_copy(r, lax.rem(me + r, n), me).start()

    widen(halo, tiles - halo)
    load_area.wait()
    mine.wait()

    @pl.when(me > 0)
    def _():
        to_right.wait_recv()

    @pl.when(me < n - 1)
    def _():
        to_left.wait_recv()

    for q in range(m):
        owner = lax.rem(t + m - q, m)
        if q:
            weights_copy(q, owner).wait_recv()
        for i in range(own):
            block = owner * own + i
            x = jnp.concatenate([ext[tidx[k, block]] for k in range(2)], axis=1).astype(jnp.bfloat16)
            nat[block] = jnp.dot(x, wall[block], preferred_element_type=jnp.float32)

    table = nat[...].reshape(blocks * frames, LANES).astype(jnp.bfloat16)

    def selected(rows, put):
        for v in range(half):
            row = jnp.concatenate([rows[v:v + 1], rows[half + v:half + v + 1]], axis=1)
            lo = row & (LANES - 1)
            hi = jnp.broadcast_to(row >> 7, (frames, 2 * LANES))
            found = jnp.dot(table, one_hot(lo), preferred_element_type=jnp.float32)
            acc = found[:frames]
            for h in range(1, blocks):
                acc = jnp.where(hi == h, found[h * frames:(h + 1) * frames], acc)
            put(v, jnp.concatenate([acc[:, :LANES], acc[:, LANES:]], axis=0).astype(jnp.bfloat16))

    rq[me] = req[me]

    @pl.loop(0, n // GROUP)
    def _(u):
        for j in range(GROUP):
            r = u * GROUP + j + 1

            @pl.when(r < n)
            def _():
                to = lax.rem(me + r, n)
                request_copy(n - r, to, to).wait_recv()

        for j in range(GROUP):
            to = lax.rem(me + u * GROUP + j + 1, n)

            def put(v, piece):
                out_buf[to, v * 16:(v + 1) * 16, :] = piece

            selected(rq[to], put)
        for j in range(GROUP):
            r = u * GROUP + j + 1

            @pl.when(r < n)
            def _():
                value_copy(r, lax.rem(me + r, n), me).start()

    vals[me] = out_buf[me]

    @pl.loop(1, n)
    def _(r):
        source = lax.rem(me + n - r, n)
        area_copy(r, source, source).wait_recv()

    @pl.loop(0, n)
    def _(s):
        rows = req[s]
        lo, hi = rows & (LANES - 1), rows >> 7
        a = areas[s].astype(jnp.float32)
        acc = jnp.zeros((8, LANES), jnp.float32)
        for h in range(blocks):
            acc = jnp.where(hi == h, pick(jnp.broadcast_to(a[h:h + 1], (8, LANES)), lo), acc)
        area_at[s] = acc

    load_slot.wait()
    load_bary.wait()

    @pl.loop(1, n)
    def _(r):
        source = lax.rem(me + n - r, n)
        value_copy(r, source, source).wait_recv()

    corners(cap, vregs, vals, area_at, slot, bary, out, tbl, packed)

    @pl.loop(1, n)
    def _(r):
        to = lax.rem(me + r, n)
        request_copy(r, to, me).wait_send()
        area_copy(r, to, me).wait_send()
        value_copy(r, to, me).wait_send()

    for q in range(1, m):
        weights_copy(q, t).wait_send()

    @pl.when(me < n - 1)
    def _():
        to_right.wait_send()

    @pl.when(me > 0)
    def _():
        to_left.wait_send()


def corners(cap, vregs, vals, area_at, slot, bary, out, tbl, packed):
    n = area_at.shape[0]
    half = vregs // 2
    frames = out.shape[0]
    entries = n * vregs
    width = 2 * LANES
    tbl[:entries * frames] = vals[...].reshape(entries * frames, LANES)
    for s in range(n):
        packed[s * vregs:(s + 1) * vregs] = area_at[s, :vregs]
    tbl[entries * frames:] = packed[...].astype(jnp.bfloat16)

    @pl.loop(0, out.shape[1] // width)
    def _(g):
        at = pl.ds(pl.multiple_of(g * width, width), width)
        top = jnp.zeros((frames, width), jnp.float32)
        total = jnp.zeros((1, width), jnp.float32)
        for k in range(3):
            flat = slot[k:k + 1, at]
            if cap == vregs * LANES:
                lo, hi = flat & (LANES - 1), flat >> 7
            else:
                source = ((flat.astype(jnp.float32) + 0.5) * (1.0 / cap)).astype(jnp.int32)
                rest = flat - source * cap
                lo, hi = rest & (LANES - 1), source * vregs + (rest >> 7)
            found = jnp.dot(tbl[...], one_hot(lo), preferred_element_type=jnp.float32)
            wide = jnp.broadcast_to(hi, (frames, width))
            acc = jnp.zeros((frames, width), jnp.float32)
            for s in range(n):
                for v in range(half):
                    for j in range(2):
                        e = (s * half + v) * 2 + j
                        here = found[e * frames:(e + 1) * frames]
                        acc = jnp.where(wide == s * vregs + j * half + v, here, acc)
            row8 = lax.broadcasted_iota(jnp.int32, (8, width), 0)
            spread = jnp.zeros((8, width), jnp.float32)
            for b in range(entries // 8):
                at8 = entries * frames + b * 8
                spread = jnp.where(wide == row8 + b * 8, found[at8:at8 + 8], spread)
            factor = bary[k:k + 1, at] * jnp.sum(spread, axis=0, keepdims=True)
            top = top + factor * acc
            total = total + factor
        out[:, at] = top / total


def shards(bold, tile_index, weights, area, requests, slot, bary):
    n, m = lax.axis_size("slab"), lax.axis_size("tm")
    frames = bold.shape[0]
    cap = requests.shape[2]
    vregs = 2 * (-(-cap // (2 * LANES)))
    own, depth, tile = weights.shape
    blocks = own * m
    message = vregs * frames
    entries = n * vregs
    vmem = pl.BlockSpec(memory_space=pltpu.VMEM)
    hbm = pl.BlockSpec(memory_space=pltpu.HBM)
    smem = pl.BlockSpec(memory_space=pltpu.SMEM)
    sem = lambda k: pltpu.SemaphoreType.DMA((k,))
    return pl.pallas_call(
        functools.partial(exchange_kernel, n, m, vregs),
        out_shape=jax.ShapeDtypeStruct((frames, slot.shape[1]), jnp.float32),
        in_specs=[smem] + [hbm] * 6,
        out_specs=vmem,
        scratch_shapes=[
            pltpu.VMEM((n, message, LANES), jnp.bfloat16),
            pltpu.VMEM((n, 8, LANES), jnp.float32),
            pltpu.VMEM((bold.shape[1] // LANES + 2 * HALO_T, frames, LANES), jnp.float32),
            pltpu.VMEM((blocks, depth, tile), jnp.bfloat16),
            pltpu.VMEM((blocks, frames, LANES), jnp.float32),
            pltpu.VMEM((n, 8, LANES), jnp.int32),
            pltpu.VMEM((n, 8, LANES), jnp.int32),
            pltpu.VMEM((n, area.shape[0] // LANES, LANES), jnp.bfloat16),
            pltpu.VMEM((n, message, LANES), jnp.bfloat16),
            pltpu.VMEM(bold.shape, jnp.bfloat16),
            pltpu.VMEM((n, cap), jnp.int32),
            pltpu.VMEM(slot.shape, jnp.int32),
            pltpu.VMEM(bary.shape, jnp.float32),
            pltpu.VMEM((entries * (frames + 1), LANES), jnp.bfloat16),
            pltpu.VMEM((entries, LANES), jnp.float32),
            sem(5), sem(2), sem(2), sem(m), sem(m), sem(n), sem(n), sem(n), sem(n), sem(n), sem(n),
        ],
        compiler_params=pltpu.CompilerParams(
            collective_id=0, has_side_effects=True),
        name="exchange",
    )(tile_index, bold, weights, area.reshape(-1, LANES), requests.reshape(n, cap), slot, bary)


def solution(mesh):
    placed = (
        P("tm", "slab"),
        P(None, "slab"),
        P(("slab", "tm"), None, None),
        P("slab"),
        P("slab", None, None),
        P(None, "slab"),
        P(None, "slab"),
    )
    return jax.shard_map(
        shards, mesh=mesh, in_specs=placed, out_specs=P("tm", "slab"), check_vma=False
    )
```

```python
import functools

import jax
import jax.numpy as jnp
from jax import lax
from jax.experimental import pallas as pl
from jax.experimental.pallas import tpu as pltpu
from jax.sharding import PartitionSpec as P

HALO_T = 8
GROUP = 4
LANES = 128
MESH = pl.DeviceIdType.MESH


def pick(table, lanes):
    return jnp.take_along_axis(table, lanes, axis=1, mode="promise_in_bounds")


def one_hot(lo, depth=LANES):
    rows = lax.broadcasted_iota(jnp.int32, (depth, lo.shape[1]), 0)
    return jnp.where(rows == lo, 1.0, 0.0).astype(jnp.bfloat16)


def exchange_kernel(n, m, vregs, tidx, bold_in, w, area, wanted_in, slot_in, bary_in, out, vals, area_at, ext, wall, nat,
                    req, rq, areas, out_buf, bold, wanted, slot, bary, tbl, packed, in_s, halo_s, halo_r, w_s, w_r, rq_s, rq_r, ar_s, ar_r, va_s, va_r):
    me = lax.axis_index("slab")
    t = lax.axis_index("tm")
    tiles = bold.shape[1] // LANES
    own = w.shape[0]
    frames = bold.shape[0]
    blocks = nat.shape[0]
    half = vregs // 2
    halo = HALO_T
    cap = wanted.shape[1]

    load_bold = pltpu.make_async_copy(bold_in, bold, in_s.at[0])
    load_wanted = pltpu.make_async_copy(wanted_in, wanted, in_s.at[1])
    load_area = pltpu.make_async_copy(area, areas.at[me], in_s.at[2])
    mine = pltpu.make_async_copy(w, wall.at[pl.ds(t * own, own)], w_s.at[0])
    load_slot = pltpu.make_async_copy(slot_in, slot, in_s.at[3])
    load_bary = pltpu.make_async_copy(bary_in, bary, in_s.at[4])
    load_bold.start()
    load_wanted.start()
    load_area.start()
    mine.start()
    load_slot.start()
    load_bary.start()
    barrier = pltpu.get_barrier_semaphore()

    @pl.loop(1, n)
    def _(r):
        pl.semaphore_signal(barrier, inc=1, device_id={"slab": lax.rem(me + r, n)}, device_id_type=MESH)

    for q in range(1, m):
        pl.semaphore_signal(barrier, inc=1, device_id={"tm": lax.rem(t + q, m)}, device_id_type=MESH)

    load_bold.wait()

    def widen(lo, hi):
        for i in range(lo, hi):
            ext[halo + i] = bold[:, i * LANES:(i + 1) * LANES].astype(jnp.float32)

    widen(0, halo)
    widen(tiles - halo, tiles)

    @pl.when(me == 0)
    def _():
        ext[0:halo] = jnp.zeros((halo, frames, LANES), jnp.float32)

    @pl.when(me == n - 1)
    def _():
        ext[halo + tiles:] = jnp.zeros((halo, frames, LANES), jnp.float32)

    load_wanted.wait()
    req[...] = jnp.zeros(req.shape, jnp.int32)
    for s in range(n):
        for v in range(vregs):
            size = min(LANES, cap - v * LANES)
            if size > 0:
                req[s, v:v + 1, 0:size] = wanted[s:s + 1, v * LANES:v * LANES + size]

    pl.semaphore_wait(barrier, n - 1 + m - 1)

    def weights_copy(q, owner):
        return pltpu.make_async_remote_copy(
            src_ref=w, dst_ref=wall.at[pl.ds(owner * own, own)],
            send_sem=w_s.at[q], recv_sem=w_r.at[q],
            device_id={"tm": lax.rem(t + q, m)}, device_id_type=MESH)

    for q in range(1, m):
        weights_copy(q, t).start()

    to_right = pltpu.make_async_remote_copy(
        src_ref=ext.at[pl.ds(tiles, halo)], dst_ref=ext.at[pl.ds(0, halo)],
        send_sem=halo_s.at[0], recv_sem=halo_r.at[0],
        device_id={"slab": lax.rem(me + 1, n)}, device_id_type=MESH)
    to_left = pltpu.make_async_remote_copy(
        src_ref=ext.at[pl.ds(halo, halo)], dst_ref=ext.at[pl.ds(halo + tiles, halo)],
        send_sem=halo_s.at[1], recv_sem=halo_r.at[1],
        device_id={"slab": lax.rem(me + n - 1, n)}, device_id_type=MESH)

    @pl.when(me < n - 1)
    def _():
        to_right.start()

    @pl.when(me > 0)
    def _():
        to_left.start()

    def request_copy(r, to, slot):
        return pltpu.make_async_remote_copy(
            src_ref=req.at[to], dst_ref=rq.at[slot], send_sem=rq_s.at[r], recv_sem=rq_r.at[r],
            device_id={"slab": to}, device_id_type=MESH)

    def area_copy(r, to, slot):
        return pltpu.make_async_remote_copy(
            src_ref=area, dst_ref=areas.at[slot], send_sem=ar_s.at[r], recv_sem=ar_r.at[r],
            device_id={"slab": to}, device_id_type=MESH)

    def value_copy(r, to, slot):
        return pltpu.make_async_remote_copy(
            src_ref=out_buf.at[to], dst_ref=vals.at[slot], send_sem=va_s.at[r], recv_sem=va_r.at[r],
            device_id={"slab": to}, device_id_type=MESH)

    @pl.loop(1, n)
    def _(r):
        request_copy(r, lax.rem(me + r, n), me).start()

    @pl.loop(1, n)
    def _(r):
        area_copy(r, lax.rem(me + r, n), me).start()

    widen(halo, tiles - halo)
    load_area.wait()
    mine.wait()

    @pl.when(me > 0)
    def _():
        to_right.wait_recv()

    @pl.when(me < n - 1)
    def _():
        to_left.wait_recv()

    for q in range(m):
        owner = lax.rem(t + m - q, m)
        if q:
            weights_copy(q, owner).wait_recv()
        for i in range(own):
            block = owner * own + i
            x = jnp.concatenate([ext[tidx[k, block]] for k in range(2)], axis=1).astype(jnp.bfloat16)
            nat[block] = jnp.dot(x, wall[block], preferred_element_type=jnp.float32)

    table = nat[...].reshape(blocks * frames, LANES).astype(jnp.bfloat16)

    def selected(rows, put):
        for v in range(half):
            row = jnp.concatenate([rows[v:v + 1], rows[half + v:half + v + 1]], axis=1)
            lo = row & (LANES - 1)
            hi = jnp.broadcast_to(row >> 7, (frames, 2 * LANES))
            found = jnp.dot(table, one_hot(lo), preferred_element_type=jnp.float32)
            acc = found[:frames]
            for h in range(1, blocks):
                acc = jnp.where(hi == h, found[h * frames:(h + 1) * frames], acc)
            put(v, jnp.concatenate([acc[:, :LANES], acc[:, LANES:]], axis=0).astype(jnp.bfloat16))

    rq[me] = req[me]

    @pl.loop(0, n // GROUP)
    def _(u):
        for j in range(GROUP):
            r = u * GROUP + j + 1

            @pl.when(r < n)
            def _():
                to = lax.rem(me + r, n)
                request_copy(n - r, to, to).wait_recv()

        for j in range(GROUP):
            to = lax.rem(me + u * GROUP + j + 1, n)

            def put(v, piece):
                out_buf[to, v * 16:(v + 1) * 16, :] = piece

            selected(rq[to], put)
        for j in range(GROUP):
            r = u * GROUP + j + 1

            @pl.when(r < n)
            def _():
                value_copy(r, lax.rem(me + r, n), me).start()

    vals[me] = out_buf[me]

    @pl.loop(1, n)
    def _(r):
        source = lax.rem(me + n - r, n)
        area_copy(r, source, source).wait_recv()

    @pl.loop(0, n)
    def _(s):
        rows = req[s]
        lo, hi = rows & (LANES - 1), rows >> 7
        a = areas[s].astype(jnp.float32)
        acc = jnp.zeros((8, LANES), jnp.float32)
        for h in range(blocks):
            acc = jnp.where(hi == h, pick(jnp.broadcast_to(a[h:h + 1], (8, LANES)), lo), acc)
        area_at[s] = acc

    load_slot.wait()
    load_bary.wait()

    @pl.loop(1, n)
    def _(r):
        source = lax.rem(me + n - r, n)
        value_copy(r, source, source).wait_recv()

    corners(cap, vregs, vals, area_at, slot, bary, out, tbl, packed)

    @pl.loop(1, n)
    def _(r):
        to = lax.rem(me + r, n)
        request_copy(r, to, me).wait_send()
        area_copy(r, to, me).wait_send()
        value_copy(r, to, me).wait_send()

    for q in range(1, m):
        weights_copy(q, t).wait_send()

    @pl.when(me < n - 1)
    def _():
        to_right.wait_send()

    @pl.when(me > 0)
    def _():
        to_left.wait_send()


def corners(cap, vregs, vals, area_at, slot, bary, out, tbl, packed):
    n = area_at.shape[0]
    half = vregs // 2
    frames = out.shape[0]
    entries = n * vregs
    width = 2 * LANES
    part = entries // 2
    top_rows = part * frames
    tbl[:top_rows, :LANES] = vals[:n // 2].reshape(top_rows, LANES)
    tbl[:top_rows, LANES:] = vals[n // 2:].reshape(top_rows, LANES)
    for s in range(n):
        packed[s * vregs:(s + 1) * vregs] = area_at[s, :vregs]
    tbl[top_rows:, :LANES] = packed[:part].astype(jnp.bfloat16)
    tbl[top_rows:, LANES:] = packed[part:].astype(jnp.bfloat16)

    @pl.loop(0, out.shape[1] // width)
    def _(g):
        at = pl.ds(pl.multiple_of(g * width, width), width)
        top = jnp.zeros((frames, width), jnp.float32)
        total = jnp.zeros((1, width), jnp.float32)
        for k in range(3):
            flat = slot[k:k + 1, at]
            if cap == vregs * LANES:
                lo, hi = flat & (LANES - 1), flat >> 7
            else:
                source = ((flat.astype(jnp.float32) + 0.5) * (1.0 / cap)).astype(jnp.int32)
                rest = flat - source * cap
                lo, hi = rest & (LANES - 1), source * vregs + (rest >> 7)
            late = hi >= part
            lo = jnp.where(late, lo + LANES, lo)
            hi = jnp.where(late, hi - part, hi)
            found = jnp.dot(tbl[...], one_hot(lo, width), preferred_element_type=jnp.float32)
            wide = jnp.broadcast_to(hi, (frames, width))
            acc = jnp.zeros((frames, width), jnp.float32)
            for s in range(n // 2):
                for v in range(half):
                    for j in range(2):
                        e = (s * half + v) * 2 + j
                        here = found[e * frames:(e + 1) * frames]
                        acc = jnp.where(wide == s * vregs + j * half + v, here, acc)
            row8 = lax.broadcasted_iota(jnp.int32, (8, width), 0)
            spread = jnp.zeros((8, width), jnp.float32)
            for b in range(part // 8):
                at8 = top_rows + b * 8
                spread = jnp.where(wide == row8 + b * 8, found[at8:at8 + 8], spread)
            factor = bary[k:k + 1, at] * jnp.sum(spread, axis=0, keepdims=True)
            top = top + factor * acc
            total = total + factor
        out[:, at] = top / total


def shards(bold, tile_index, weights, area, requests, slot, bary):
    n, m = lax.axis_size("slab"), lax.axis_size("tm")
    frames = bold.shape[0]
    cap = requests.shape[2]
    vregs = 2 * (-(-cap // (2 * LANES)))
    own, depth, tile = weights.shape
    blocks = own * m
    message = vregs * frames
    entries = n * vregs
    vmem = pl.BlockSpec(memory_space=pltpu.VMEM)
    hbm = pl.BlockSpec(memory_space=pltpu.HBM)
    smem = pl.BlockSpec(memory_space=pltpu.SMEM)
    sem = lambda k: pltpu.SemaphoreType.DMA((k,))
    return pl.pallas_call(
        functools.partial(exchange_kernel, n, m, vregs),
        out_shape=jax.ShapeDtypeStruct((frames, slot.shape[1]), jnp.float32),
        in_specs=[smem] + [hbm] * 6,
        out_specs=vmem,
        scratch_shapes=[
            pltpu.VMEM((n, message, LANES), jnp.bfloat16),
            pltpu.VMEM((n, 8, LANES), jnp.float32),
            pltpu.VMEM((bold.shape[1] // LANES + 2 * HALO_T, frames, LANES), jnp.float32),
            pltpu.VMEM((blocks, depth, tile), jnp.bfloat16),
            pltpu.VMEM((blocks, frames, LANES), jnp.float32),
            pltpu.VMEM((n, 8, LANES), jnp.int32),
            pltpu.VMEM((n, 8, LANES), jnp.int32),
            pltpu.VMEM((n, area.shape[0] // LANES, LANES), jnp.bfloat16),
            pltpu.VMEM((n, message, LANES), jnp.bfloat16),
            pltpu.VMEM(bold.shape, jnp.bfloat16),
            pltpu.VMEM((n, cap), jnp.int32),
            pltpu.VMEM(slot.shape, jnp.int32),
            pltpu.VMEM(bary.shape, jnp.float32),
            pltpu.VMEM((entries // 2 * (frames + 1), 2 * LANES), jnp.bfloat16),
            pltpu.VMEM((entries, LANES), jnp.float32),
            sem(5), sem(2), sem(2), sem(m), sem(m), sem(n), sem(n), sem(n), sem(n), sem(n), sem(n),
        ],
        compiler_params=pltpu.CompilerParams(
            collective_id=0, has_side_effects=True),
        name="exchange",
    )(tile_index, bold, weights, area.reshape(-1, LANES), requests.reshape(n, cap), slot, bary)


def solution(mesh):
    placed = (
        P("tm", "slab"),
        P(None, "slab"),
        P(("slab", "tm"), None, None),
        P("slab"),
        P("slab", None, None),
        P(None, "slab"),
        P(None, "slab"),
    )
    return jax.shard_map(
        shards, mesh=mesh, in_specs=placed, out_specs=P("tm", "slab"), check_vma=False
    )
```

```python
import functools

import jax
import jax.numpy as jnp
from jax import lax
from jax.experimental import pallas as pl
from jax.experimental.pallas import tpu as pltpu
from jax.sharding import PartitionSpec as P

HALO_T = 8
GROUP = 4
LANES = 128
MESH = pl.DeviceIdType.MESH


def pick(table, lanes):
    return jnp.take_along_axis(table, lanes, axis=1, mode="promise_in_bounds")


def one_hot(lo, depth=LANES):
    rows = lax.broadcasted_iota(jnp.int32, (depth, lo.shape[1]), 0)
    return jnp.where(rows == lo, 1.0, 0.0).astype(jnp.bfloat16)


def exchange_kernel(n, m, vregs, tidx, bold_in, w, area, wanted_in, slot_in, bary_in, out, vals, area_at, ext, wall, nat,
                    req, rq, areas, out_buf, bold, wanted, slot, bary, tbl, packed, in_s, halo_s, halo_r, w_s, w_r, rq_s, rq_r, ar_s, ar_r, va_s, va_r):
    me = lax.axis_index("slab")
    t = lax.axis_index("tm")
    tiles = bold.shape[1] // LANES
    own = w.shape[0]
    frames = bold.shape[0]
    blocks = nat.shape[0]
    half = vregs // 2
    halo = HALO_T
    cap = wanted.shape[1]

    load_bold = pltpu.make_async_copy(bold_in, bold, in_s.at[0])
    load_wanted = pltpu.make_async_copy(wanted_in, wanted, in_s.at[1])
    load_area = pltpu.make_async_copy(area, areas.at[me], in_s.at[2])
    mine = pltpu.make_async_copy(w, wall.at[pl.ds(t * own, own)], w_s.at[0])
    load_slot = pltpu.make_async_copy(slot_in, slot, in_s.at[3])
    load_bary = pltpu.make_async_copy(bary_in, bary, in_s.at[4])
    load_bold.start()
    load_wanted.start()
    load_area.start()
    mine.start()
    load_slot.start()
    load_bary.start()
    barrier = pltpu.get_barrier_semaphore()

    @pl.loop(1, n)
    def _(r):
        pl.semaphore_signal(barrier, inc=1, device_id={"slab": lax.rem(me + r, n)}, device_id_type=MESH)

    for q in range(1, m):
        pl.semaphore_signal(barrier, inc=1, device_id={"tm": lax.rem(t + q, m)}, device_id_type=MESH)

    load_bold.wait()

    def widen(lo, hi):
        for i in range(lo, hi):
            ext[halo + i] = bold[:, i * LANES:(i + 1) * LANES].astype(jnp.float32)

    widen(0, halo)
    widen(tiles - halo, tiles)

    @pl.when(me == 0)
    def _():
        ext[0:halo] = jnp.zeros((halo, frames, LANES), jnp.float32)

    @pl.when(me == n - 1)
    def _():
        ext[halo + tiles:] = jnp.zeros((halo, frames, LANES), jnp.float32)

    load_wanted.wait()
    req[...] = jnp.zeros(req.shape, jnp.int32)
    for s in range(n):
        for v in range(vregs):
            size = min(LANES, cap - v * LANES)
            if size > 0:
                req[s, v:v + 1, 0:size] = wanted[s:s + 1, v * LANES:v * LANES + size]

    pl.semaphore_wait(barrier, n - 1 + m - 1)

    def weights_copy(q, owner):
        return pltpu.make_async_remote_copy(
            src_ref=w, dst_ref=wall.at[pl.ds(owner * own, own)],
            send_sem=w_s.at[q], recv_sem=w_r.at[q],
            device_id={"tm": lax.rem(t + q, m)}, device_id_type=MESH)

    for q in range(1, m):
        weights_copy(q, t).start()

    to_right = pltpu.make_async_remote_copy(
        src_ref=ext.at[pl.ds(tiles, halo)], dst_ref=ext.at[pl.ds(0, halo)],
        send_sem=halo_s.at[0], recv_sem=halo_r.at[0],
        device_id={"slab": lax.rem(me + 1, n)}, device_id_type=MESH)
    to_left = pltpu.make_async_remote_copy(
        src_ref=ext.at[pl.ds(halo, halo)], dst_ref=ext.at[pl.ds(halo + tiles, halo)],
        send_sem=halo_s.at[1], recv_sem=halo_r.at[1],
        device_id={"slab": lax.rem(me + n - 1, n)}, device_id_type=MESH)

    @pl.when(me < n - 1)
    def _():
        to_right.start()

    @pl.when(me > 0)
    def _():
        to_left.start()

    def request_copy(r, to, slot):
        return pltpu.make_async_remote_copy(
            src_ref=req.at[to], dst_ref=rq.at[slot], send_sem=rq_s.at[r], recv_sem=rq_r.at[r],
            device_id={"slab": to}, device_id_type=MESH)

    def area_copy(r, to, slot):
        return pltpu.make_async_remote_copy(
            src_ref=area, dst_ref=areas.at[slot], send_sem=ar_s.at[r], recv_sem=ar_r.at[r],
            device_id={"slab": to}, device_id_type=MESH)

    def value_copy(r, to, slot):
        return pltpu.make_async_remote_copy(
            src_ref=out_buf.at[to], dst_ref=vals.at[slot], send_sem=va_s.at[r], recv_sem=va_r.at[r],
            device_id={"slab": to}, device_id_type=MESH)

    @pl.loop(1, n)
    def _(r):
        request_copy(r, lax.rem(me + r, n), me).start()

    @pl.loop(1, n)
    def _(r):
        area_copy(r, lax.rem(me + r, n), me).start()

    widen(halo, tiles - halo)
    load_area.wait()
    mine.wait()

    @pl.when(me > 0)
    def _():
        to_right.wait_recv()

    @pl.when(me < n - 1)
    def _():
        to_left.wait_recv()

    for q in range(m):
        owner = lax.rem(t + m - q, m)
        if q:
            weights_copy(q, owner).wait_recv()
        for i in range(own):
            block = owner * own + i
            x = jnp.concatenate([ext[tidx[k, block]] for k in range(2)], axis=1).astype(jnp.bfloat16)
            nat[block] = jnp.dot(x, wall[block], preferred_element_type=jnp.float32)

    part = blocks // 2
    table = jnp.concatenate(
        [nat[:part].reshape(part * frames, LANES), nat[part:].reshape(part * frames, LANES)], axis=1
    ).astype(jnp.bfloat16)

    def selected(rows, put):
        for v in range(half):
            row = jnp.concatenate([rows[v:v + 1], rows[half + v:half + v + 1]], axis=1)
            lo = row & (LANES - 1)
            hi = row >> 7
            late = hi >= part
            lo = jnp.where(late, lo + LANES, lo)
            hi = jnp.broadcast_to(jnp.where(late, hi - part, hi), (frames, 2 * LANES))
            found = jnp.dot(table, one_hot(lo, 2 * LANES), preferred_element_type=jnp.float32)
            acc = found[:frames]
            for h in range(1, part):
                acc = jnp.where(hi == h, found[h * frames:(h + 1) * frames], acc)
            put(v, jnp.concatenate([acc[:, :LANES], acc[:, LANES:]], axis=0).astype(jnp.bfloat16))

    rq[me] = req[me]

    @pl.loop(0, n // GROUP)
    def _(u):
        for j in range(GROUP):
            r = u * GROUP + j + 1

            @pl.when(r < n)
            def _():
                to = lax.rem(me + r, n)
                request_copy(n - r, to, to).wait_recv()

        for j in range(GROUP):
            to = lax.rem(me + u * GROUP + j + 1, n)

            def put(v, piece):
                out_buf[to, v * 16:(v + 1) * 16, :] = piece

            selected(rq[to], put)
        for j in range(GROUP):
            r = u * GROUP + j + 1

            @pl.when(r < n)
            def _():
                value_copy(r, lax.rem(me + r, n), me).start()

    vals[me] = out_buf[me]

    @pl.loop(1, n)
    def _(r):
        source = lax.rem(me + n - r, n)
        area_copy(r, source, source).wait_recv()

    @pl.loop(0, n)
    def _(s):
        rows = req[s]
        lo, hi = rows & (LANES - 1), rows >> 7
        a = areas[s].astype(jnp.float32)
        acc = jnp.zeros((8, LANES), jnp.float32)
        for h in range(blocks):
            acc = jnp.where(hi == h, pick(jnp.broadcast_to(a[h:h + 1], (8, LANES)), lo), acc)
        area_at[s] = acc

    load_slot.wait()
    load_bary.wait()

    @pl.loop(1, n)
    def _(r):
        source = lax.rem(me + n - r, n)
        value_copy(r, source, source).wait_recv()

    corners(cap, vregs, vals, area_at, slot, bary, out, tbl, packed)

    @pl.loop(1, n)
    def _(r):
        to = lax.rem(me + r, n)
        request_copy(r, to, me).wait_send()
        area_copy(r, to, me).wait_send()
        value_copy(r, to, me).wait_send()

    for q in range(1, m):
        weights_copy(q, t).wait_send()

    @pl.when(me < n - 1)
    def _():
        to_right.wait_send()

    @pl.when(me > 0)
    def _():
        to_left.wait_send()


def corners(cap, vregs, vals, area_at, slot, bary, out, tbl, packed):
    n = area_at.shape[0]
    half = vregs // 2
    frames = out.shape[0]
    entries = n * vregs
    width = 2 * LANES
    part = entries // 2
    top_rows = part * frames
    tbl[:top_rows, :LANES] = vals[:n // 2].reshape(top_rows, LANES)
    tbl[:top_rows, LANES:] = vals[n // 2:].reshape(top_rows, LANES)
    for s in range(n):
        packed[s * vregs:(s + 1) * vregs] = area_at[s, :vregs]
    tbl[top_rows:, :LANES] = packed[:part].astype(jnp.bfloat16)
    tbl[top_rows:, LANES:] = packed[part:].astype(jnp.bfloat16)

    @pl.loop(0, out.shape[1] // width, unroll=2)
    def _(g):
        at = pl.ds(pl.multiple_of(g * width, width), width)
        top = jnp.zeros((frames, width), jnp.float32)
        total = jnp.zeros((1, width), jnp.float32)
        for k in range(3):
            flat = slot[k:k + 1, at]
            if cap == vregs * LANES:
                lo, hi = flat & (LANES - 1), flat >> 7
            else:
                source = ((flat.astype(jnp.float32) + 0.5) * (1.0 / cap)).astype(jnp.int32)
                rest = flat - source * cap
                lo, hi = rest & (LANES - 1), source * vregs + (rest >> 7)
            late = hi >= part
            lo = jnp.where(late, lo + LANES, lo)
            hi = jnp.where(late, hi - part, hi)
            found = jnp.dot(tbl[...], one_hot(lo, width), preferred_element_type=jnp.float32)
            wide = jnp.broadcast_to(hi, (frames, width))
            acc = jnp.zeros((frames, width), jnp.float32)
            for s in range(n // 2):
                for v in range(half):
                    for j in range(2):
                        e = (s * half + v) * 2 + j
                        here = found[e * frames:(e + 1) * frames]
                        acc = jnp.where(wide == s * vregs + j * half + v, here, acc)
            row8 = lax.broadcasted_iota(jnp.int32, (8, width), 0)
            spread = jnp.zeros((8, width), jnp.float32)
            for b in range(part // 8):
                at8 = top_rows + b * 8
                spread = jnp.where(wide == row8 + b * 8, found[at8:at8 + 8], spread)
            factor = bary[k:k + 1, at] * jnp.sum(spread, axis=0, keepdims=True)
            top = top + factor * acc
            total = total + factor
        out[:, at] = top / total


def shards(bold, tile_index, weights, area, requests, slot, bary):
    n, m = lax.axis_size("slab"), lax.axis_size("tm")
    frames = bold.shape[0]
    cap = requests.shape[2]
    vregs = 2 * (-(-cap // (2 * LANES)))
    own, depth, tile = weights.shape
    blocks = own * m
    message = vregs * frames
    entries = n * vregs
    vmem = pl.BlockSpec(memory_space=pltpu.VMEM)
    hbm = pl.BlockSpec(memory_space=pltpu.HBM)
    smem = pl.BlockSpec(memory_space=pltpu.SMEM)
    sem = lambda k: pltpu.SemaphoreType.DMA((k,))
    return pl.pallas_call(
        functools.partial(exchange_kernel, n, m, vregs),
        out_shape=jax.ShapeDtypeStruct((frames, slot.shape[1]), jnp.float32),
        in_specs=[smem] + [hbm] * 6,
        out_specs=vmem,
        scratch_shapes=[
            pltpu.VMEM((n, message, LANES), jnp.bfloat16),
            pltpu.VMEM((n, 8, LANES), jnp.float32),
            pltpu.VMEM((bold.shape[1] // LANES + 2 * HALO_T, frames, LANES), jnp.float32),
            pltpu.VMEM((blocks, depth, tile), jnp.bfloat16),
            pltpu.VMEM((blocks, frames, LANES), jnp.float32),
            pltpu.VMEM((n, 8, LANES), jnp.int32),
            pltpu.VMEM((n, 8, LANES), jnp.int32),
            pltpu.VMEM((n, area.shape[0] // LANES, LANES), jnp.bfloat16),
            pltpu.VMEM((n, message, LANES), jnp.bfloat16),
            pltpu.VMEM(bold.shape, jnp.bfloat16),
            pltpu.VMEM((n, cap), jnp.int32),
            pltpu.VMEM(slot.shape, jnp.int32),
            pltpu.VMEM(bary.shape, jnp.float32),
            pltpu.VMEM((entries // 2 * (frames + 1), 2 * LANES), jnp.bfloat16),
            pltpu.VMEM((entries, LANES), jnp.float32),
            sem(5), sem(2), sem(2), sem(m), sem(m), sem(n), sem(n), sem(n), sem(n), sem(n), sem(n),
        ],
        compiler_params=pltpu.CompilerParams(
            collective_id=0, has_side_effects=True),
        name="exchange",
    )(tile_index, bold, weights, area.reshape(-1, LANES), requests.reshape(n, cap), slot, bary)


def solution(mesh):
    placed = (
        P("tm", "slab"),
        P(None, "slab"),
        P(("slab", "tm"), None, None),
        P("slab"),
        P("slab", None, None),
        P(None, "slab"),
        P(None, "slab"),
    )
    return jax.shard_map(
        shards, mesh=mesh, in_specs=placed, out_specs=P("tm", "slab"), check_vma=False
    )
```
